256 devices in a mesh: dp: 16 (over z, y_lo), blk: 16 (over y_hi, x, core).
Axes of the slice: x: 4, y: 4 (y_hi: 2, y_lo: 2; y = y_hi * 2 + y_lo), z: 8, core: 2. Of those that a mesh axis runs over, the one named last changes fastest.
Arguments:
- images: bfloat16 [98304, 1152], P(('dp', 'blk')), may hold values from -0.1875 to 0.1875
- texts: bfloat16 [32768, 1152], P(('dp', 'blk')), may hold values from -0.1875 to 0.1875
- owners: int32 [98304, 1], P(('dp', 'blk')), may hold values from 0 to 15; in each aligned block of 384 rows (0 to 383, 384 to 767, ...) at most 48 rows name the same one
- labels: int32 [98304], P(('dp', 'blk')), may hold values from 0 to 127
- counts: int32 [256], P(('dp', 'blk')), may hold values from 288 to 384, as said below
- scale: float32 [1], replicated, may hold values from 10 to 30
- bias: float32 [1], replicated, may hold values from -4 to -2
Outputs:
- image_grads: bfloat16 [98304, 1152], P(('dp', 'blk'))
- row_loss: bfloat16 [98304], P(('dp', 'blk'))
- text_grads: bfloat16 [32768, 1152], P(('dp', 'blk'))
The draws below stay inside these ranges and needn't reach their ends.
Inputs may be any that keep to these rules, and one draw needn't show every extreme that they name: `owners`: among one device's 384 rows no owner is named by more than 48 rows, a bound that some block reaches. `counts`: the live rows are the first ones of each pack; some pack is full in every draw.
All inputs are finite; a program needn't handle non-finite values.
Results may differ from the reference program's by a relative error of at most 0.0065.
Values may be sent and summed in bfloat16 or wider, within the bound.
A program may use at most 64 MiB of HBM per device.

```python
import math
import jax
import jax.numpy as jnp
import numpy as np
from jax import lax

D = 1152
PACK = 384
ROWS = 128
CAP = 48
SLOTS = 768
GROWS = 98304
TEXTS = 32768
N_DP = 16
N_BLK = 16
DEVICES = 256


def draw_counts(key, part):
    key = jax.random.fold_in(key, 11)
    first, second = jax.random.split(key)
    values = jax.random.randint(first, (DEVICES,), 3 * PACK // 4, PACK + 1)
    chosen = jax.random.randint(second, (), 0, DEVICES)
    return values.at[chosen].set(PACK).astype(jnp.int32)


def touch_ends(array, own_key, least, largest):
    longest = array.shape.index(max(array.shape))
    spots = []
    for shift in (0, 1):
        where = [jax.random.randint(jax.random.fold_in(own_key, axis), (), 0, length) for axis, length in enumerate(array.shape)]
        where[longest] = (where[longest] + shift) % array.shape[longest]
        spots.append(tuple(where))
    return array.at[spots[0]].set(least).at[spots[1]].set(largest)


def steps_of(own_key, shape, cuts, smallest, largest):
    def one(position, parts):
        heights = jax.random.uniform(jax.random.fold_in(jax.random.fold_in(own_key, 6), position), (parts,), jnp.float32, smallest / len(cuts), largest / len(cuts))
        return jnp.repeat(jnp.exp(heights), shape[position] // parts).reshape((-1,) + (1,) * (len(shape) - position - 1))

    gain = one(*cuts[0])
    for cut in cuts[1:]:
        gain = gain * one(*cut)
    return gain


def routed_block(own_key, own, number, rows, count, top, limit, slope):
    ranking = jax.random.permutation(own_key, count)
    crowded, common = load_shares(count, rows * top, limit, slope, True), load_shares(count, rows * top, limit, slope, False)
    places = jnp.arange(count)

    def named(lengths, turn):
        used = int((lengths > 0).sum())
        fixed = max(1, used // 4)
        passed = fixed + (places - fixed + turn * (used - fixed)) % max(1, count - fixed)
        return jnp.zeros((count,), jnp.int32).at[ranking[jnp.where(places < fixed, places, passed)]].set(jnp.asarray(lengths, jnp.int32))

    lengths = jnp.where(number % 4 == 0, named(crowded, number // 4), named(common, number - number // 4 - 1))
    mixed = jax.random.permutation(jax.random.fold_in(own, 3), count)
    donor, sink = mixed[0:count // 2 * 2:2], mixed[1:count // 2 * 2:2]
    room = jnp.minimum(lengths[donor] - 1, limit - lengths[sink]) // 2
    room = jnp.where((donor == ranking[0]) | (sink == ranking[0]) | (lengths[sink] == 0), 0, jnp.maximum(room, 0))
    passed = jax.random.randint(jax.random.fold_in(own, 4), (count // 2,), 0, 1 << 20) % (room + 1)
    lengths = lengths.at[donor].add(-passed).at[sink].add(passed)
    members = jnp.searchsorted(jnp.cumsum(lengths), jnp.arange(rows * top), side="right").astype(jnp.int32)
    table = members.reshape(top, rows).T
    table = table[jax.random.permutation(jax.random.fold_in(own, 1), rows)]
    turn = jax.random.randint(jax.random.fold_in(own, 2), (rows, 1), 0, top)
    return jnp.take_along_axis(table, (jnp.arange(top)[None, :] + turn) % top, axis=1)


def load_shares(number_of, total, reach, slope, full):
    portions = [(1 << 20) // math.isqrt(standing ** slope) + 1 for standing in range(1, number_of + 1)]
    largest = reach if full else min(reach, max(-(-total // number_of), total * portions[0] // sum(portions)))
    least = 1 if total - largest >= number_of - 1 else 0
    holding, spare = [largest] + [least] * (number_of - 1), total - largest - least * (number_of - 1)
    while spare > 0:
        candidates = [i for i in range(1, number_of) if holding[i] < largest] or [i for i in range(1, number_of) if holding[i] < reach]
        pool, left = sum([portions[i] for i in candidates]), spare
        for i in candidates:
            more = min(reach - holding[i], max(1, left * portions[i] // pool), spare)
            holding[i] = holding[i] + more
            spare = spare - more
    return np.array(holding)


def bell_draw(key, shape, spread, reach, cuts=(), held_as=jnp.bfloat16):
    level = steps_of(key, shape, cuts, -0.22, 0.18) if cuts else 1.0
    drawn = jax.random.normal(key, shape, jnp.float32) * spread * level
    return jnp.minimum(jnp.maximum(drawn, -reach), reach).astype(held_as)


def setup_inputs(seed: int = 0) -> dict:
    streams_of = jax.random.split(jax.random.key(seed), 8)
    images = bell_draw(streams_of[0], (GROWS, D), 0.03, 0.1875, ((0, 256),))
    texts = bell_draw(streams_of[1], (TEXTS, D), 0.03, 0.1875, ((0, 256),))
    owners_keys = jax.random.split(jax.random.fold_in(streams_of[2], 1), GROWS // PACK)
    owners_turns = jax.random.permutation(jax.random.fold_in(streams_of[2], 3), GROWS // PACK)
    owners = jax.vmap(lambda own, number: routed_block(jax.random.fold_in(streams_of[2], 2), own, number, PACK, N_DP, 1, CAP, 2))(owners_keys, owners_turns).reshape((GROWS, 1))
    labels = touch_ends(jax.random.randint(streams_of[3], (GROWS,), 0, ROWS), jax.random.fold_in(streams_of[3], 1), 0, ROWS - 1).astype(jnp.int32)
    counts = draw_counts(jax.random.fold_in(streams_of[7], 71), 0)
    scale = jnp.clip(jnp.exp(jax.random.uniform(streams_of[5], (1,), jnp.float32, math.log(10.0), math.log(30.0))), 10.0, 30.0)
    bias = jnp.clip(jax.random.uniform(streams_of[6], (1,), jnp.float32, -4.0, -2.0), -4.0, -2.0)
    return dict(images=images, texts=texts, owners=owners, labels=labels, counts=counts, scale=scale, bias=bias)


def normalize(rows):
    wide = rows.astype(jnp.float32)
    inv = lax.rsqrt(lax.optimization_barrier(jnp.sum(wide * wide, axis=1, keepdims=True)) + 1e-06)
    return (wide * inv, inv)

def unnormalize(unit, inv, grad):
    return (inv * (grad - unit * lax.optimization_barrier(jnp.sum(unit * grad, axis=1, keepdims=True)))).astype(jnp.bfloat16)

def weigh(units, block, wanted, present, hit, temper, offset):
    logits = temper * lax.dot_general(units, block, (((1,), (1,)), ((), ())), preferred_element_type=jnp.float32) + offset
    columns = lax.broadcasted_iota(jnp.int32, logits.shape, 1)
    positive = (columns == wanted[:, None]) & present[:, None] & hit
    sign = jnp.where(positive, 1.0, -1.0).astype(jnp.float32)
    margin = sign * logits
    weight = jnp.where(present[:, None], 1.0, 0.0).astype(jnp.float32)
    losses = lax.optimization_barrier(jnp.sum(jax.nn.softplus(-margin) * weight, axis=1))
    coef = (-sign * jax.nn.sigmoid(-margin) * temper * weight).astype(jnp.bfloat16)
    return (losses, coef)

def reference(images, texts, owners, labels, counts, scale, bias):
    depth = N_DP
    cycle = N_BLK
    devices = depth * cycle
    temper = scale[0]
    offset = bias[0]
    dest = owners[:, 0].reshape(devices, PACK)
    live = jnp.arange(PACK, dtype=jnp.int32)[None, :] < counts[:, None]
    onehot = ((dest[:, :, None] == jnp.arange(depth, dtype=jnp.int32)[None, None, :]) & live[:, :, None]).astype(jnp.int32)
    before = jnp.cumsum(onehot, axis=1) - onehot
    place = lax.optimization_barrier(jnp.sum(before * onehot, axis=2)).astype(jnp.int32)
    source = (jnp.arange(devices, dtype=jnp.int32) // cycle)[:, None]
    column = (jnp.arange(devices, dtype=jnp.int32) % cycle)[:, None]
    target = ((dest * cycle + column) * SLOTS + source * CAP + place).astype(jnp.int32)
    outside = devices * SLOTS
    target = jnp.where(live, target, outside).reshape(-1)
    live_flat = live.reshape(-1)
    received = jnp.zeros((outside, D), jnp.bfloat16).at[target].set(images, mode='drop')
    tags = jnp.zeros((outside,), jnp.int32).at[target].set(labels + 1, mode='drop')
    received = received.reshape(depth, cycle, SLOTS, D)
    tags = tags.reshape(depth, cycle, SLOTS)
    grouped = texts.reshape(depth, cycle * ROWS, D)

    def group(packed):
        rows_in, tag_rows, text_rows = packed
        text_units, text_inv = normalize(text_rows)
        text_b = text_units.astype(jnp.bfloat16)

        def owner(total, item):
            block_rows, tag_row, index = item
            units, inv = normalize(block_rows)
            unit_b = units.astype(jnp.bfloat16)
            present = tag_row > 0
            wanted = index * ROWS + tag_row - 1
            losses, coef = weigh(unit_b, text_b, wanted, present, True, temper, offset)
            image_sum = jnp.dot(coef, text_b, preferred_element_type=jnp.float32)
            text_part = lax.dot_general(coef, unit_b, (((0,), (0,)), ((), ())), preferred_element_type=jnp.float32)
            return (total + text_part, (unnormalize(units, inv, image_sum), (losses / (cycle * ROWS)).astype(jnp.bfloat16)))
        start = jnp.zeros((cycle * ROWS, D), jnp.float32)
        total, (grads, losses) = lax.scan(owner, start, (rows_in, tag_rows, jnp.arange(cycle, dtype=jnp.int32)))
        return (grads, losses, unnormalize(text_units, text_inv, total))
    grads, losses, text_out = lax.map(group, (received, tags, grouped))
    grads = grads.reshape(outside, D)
    losses = losses.reshape(outside)
    pick = jnp.minimum(target, outside - 1)
    image_grads = jnp.where(live_flat[:, None], grads[pick], jnp.zeros((), jnp.bfloat16)).astype(jnp.bfloat16)
    row_loss = jnp.where(live_flat, losses[pick], jnp.zeros((), jnp.bfloat16)).astype(jnp.bfloat16)
    return (image_grads, row_loss, text_out.reshape(depth * cycle * ROWS, D))
```

```python
import functools

import jax
import jax.numpy as jnp
from jax import lax
from jax.experimental import pallas as pl
from jax.experimental.pallas import tpu as pltpu
from jax.sharding import PartitionSpec as P

MESH = pl.DeviceIdType.MESH
BF16 = jnp.bfloat16
F32 = jnp.float32
EPS = 1e-06

NZ, NY, NH, NX = 8, 2, 2, 4
PACK = 384
ROWS = 128
CAP = 48
BUCKETS = 16
SLOTS = CAP * BUCKETS
WIDTH = 1152
TEXTS = 2048
GROUP = 256
GROUPS = SLOTS // GROUP
TILE = 512
TILES = TEXTS // TILE

ORDER = (
    (4, 0), (4, 1), (3, 0), (5, 0), (3, 1),
    (5, 1), (2, 0), (6, 0), (2, 1), (6, 1),
    (1, 0), (7, 0), (1, 1), (7, 1), (0, 1), (0, 0),
)
SELF = BUCKETS - 1


def place_of():
    p, c = lax.axis_index("dp"), lax.axis_index("blk")
    return p // NY, p % NY, c // (2 * NX), (c // 2) % NX, c % 2


def peer(dz=0, dy=0, dh=0, dx=0, dc=0):
    z, y, h, x, core = place_of()
    return (
        ((z + dz) % NZ) * NY + (y + dy) % NY,
        (((h + dh) % NH) * NX + (x + dx) % NX) * 2 + (core + dc) % 2,
    )


def block_index(dh, dx, dc):
    return (dh * NX + dx) * 2 + dc


def dot(a, b, dims):
    return lax.dot_general(a, b, ((dims[:1], dims[1:]), ((), ())), preferred_element_type=F32)


def spread():
    lane = lax.broadcasted_iota(jnp.int32, (128, SLOTS), 1)
    row = lax.broadcasted_iota(jnp.int32, (128, SLOTS), 0)
    return jnp.where(lane % CAP == row, 1.0, 0.0).astype(BF16)


def own_lanes(every):
    lane = lax.broadcasted_iota(jnp.int32, (128, SLOTS), 1)
    row = lax.broadcasted_iota(jnp.int32, (128, SLOTS), 0)
    own = lane // CAP == row // 8
    return own if every else own & (row % 8 == 0)


def pack_row(row, spreader):
    kept = jnp.where(own_lanes(True), row, 0.0).astype(BF16)
    return dot(kept, spreader, (1, 1)).reshape(BUCKETS, 8, 128)


def unpack_row(tiles, spreader):
    wide = dot(tiles.reshape(128, 128).astype(BF16), spreader, (1, 0))
    return jnp.sum(jnp.where(own_lanes(False), wide, 0.0), axis=0, keepdims=True)


def kernel(
    img_ref, txt_ref, own_ref, lab_ref, cnt_ref, scale_ref, bias_ref,
    grad_ref, loss_ref, tgrad_ref,
    pick_ref, out_ref, recv_ref, unit_ref, gsend_ref, back_ref,
    tagsend_ref, tagrecv_ref, losssend_ref, lossback_ref,
    texts_ref, tsum_ref, isum_ref, lsum_ref, inv_ref,
    sibsend_ref, sibrecv_ref, xsend_ref, xrecv_ref, ysend_ref, yrecv_ref,
    img_sems, tag_sems, back_sems, lback_sems, txt_sems, sib_sems, x_sems, y_sems,
):
    temper, offset, live_rows = scale_ref[0], bias_ref[0], cnt_ref[0]

    barrier = pltpu.get_barrier_semaphore()
    greeted = [peer(dz=dz, dy=dy) for dz, dy in ORDER[:SELF]]
    greeted += [peer(dc=1), peer(dh=1), peer(dx=1), peer(dx=2), peer(dx=3)]
    for device in greeted:
        pl.semaphore_signal(barrier, inc=1, device_id=device, device_id_type=MESH)

    def remote(src, dst, sems, index, device):
        return pltpu.make_async_remote_copy(
            src_ref=src,
            dst_ref=dst,
            send_sem=sems.at[0, index],
            recv_sem=sems.at[1, index],
            device_id=device,
            device_id_type=MESH,
        )

    bucket = lax.broadcasted_iota(jnp.int32, (BUCKETS, PACK), 0)
    owner_of = jnp.zeros((BUCKETS, PACK), jnp.int32)
    for o, (dz, dy) in enumerate(ORDER):
        owner_of = jnp.where(bucket == o, peer(dz=dz, dy=dy)[0], owner_of)
    live = lax.broadcasted_iota(jnp.int32, (BUCKETS, PACK), 1) < live_rows
    onehot = jnp.where((own_ref[...] == owner_of) & live, 1.0, 0.0)
    earlier = jnp.where(
        lax.broadcasted_iota(jnp.int32, (PACK, PACK), 0)
        < lax.broadcasted_iota(jnp.int32, (PACK, PACK), 1),
        1.0,
        0.0,
    ).astype(BF16)
    before = dot(onehot.astype(BF16), earlier, (1, 0))
    target = jnp.sum(onehot * (before + (bucket * CAP + 1).astype(F32)), axis=0, keepdims=True)
    target = target.astype(jnp.int32) - 1
    slot = lax.broadcasted_iota(jnp.int32, (SLOTS, PACK), 0)
    pick_ref[...] = jnp.where(slot == target, 1.0, 0.0).astype(BF16)
    spreader = spread()
    tags = dot(
        jnp.broadcast_to((lab_ref[...] + 1).astype(F32), (8, PACK)).astype(BF16), pick_ref[...], (1, 1)
    )
    tagsend_ref[...] = pack_row(tags[0:1], spreader)
    tagrecv_ref[SELF] = tagsend_ref[SELF]

    img_copies = [
        remote(
            out_ref.at[pl.ds(CAP * o, CAP)], recv_ref.at[pl.ds(CAP * o, CAP)], img_sems, o,
            peer(dz=ORDER[o][0], dy=ORDER[o][1]),
        )
        for o in range(SELF)
    ]
    tag_copies = [
        remote(
            tagsend_ref.at[o], tagrecv_ref.at[o], tag_sems, o, peer(dz=ORDER[o][0], dy=ORDER[o][1])
        )
        for o in range(SELF)
    ]
    pl.semaphore_wait(barrier, len(greeted))
    for copy in tag_copies:
        copy.start()
    for g in range(GROUPS):
        rows = pl.ds(g * GROUP, GROUP)
        out_ref[rows, :] = dot(pick_ref[rows, :], img_ref[...], (1, 0)).astype(BF16)
        for o in range(BUCKETS):
            end = (o + 1) * CAP
            if g * GROUP < end <= (g + 1) * GROUP and o != SELF:
                img_copies[o].start()
    kept = pl.ds(SELF * CAP, CAP)
    recv_ref[kept, :] = out_ref[kept, :]

    wide = txt_ref[...].astype(F32)
    texts_ref[pl.ds(0, ROWS), :] = (
        wide * lax.rsqrt(jnp.sum(wide * wide, axis=1, keepdims=True) + EPS)
    ).astype(BF16)

    def text_copy(dh, dx, dc):
        if dc:
            source, device = (dh, dx, 0), peer(dc=1)
        elif dx:
            source, device = (dh, 0, 0), peer(dx=-dx)
        else:
            source, device = (0, 0, 0), peer(dh=1)
        j, i = block_index(dh, dx, dc), block_index(*source)
        return remote(
            texts_ref.at[pl.ds(ROWS * i, ROWS)], texts_ref.at[pl.ds(ROWS * j, ROWS)], txt_sems, j, device
        )

    near = (1, 3, 2)
    text_copies = {
        (dh, dx, dc): text_copy(dh, dx, dc)
        for dh in range(NH)
        for dx in range(NX)
        for dc in range(2)
        if (dh, dx, dc) != (0, 0, 0)
    }
    text_copies[1, 0, 0].start()
    for dx in near:
        text_copies[0, dx, 0].start()
    text_copies[0, 0, 1].start()
    text_copies[1, 0, 0].wait_recv()
    for dx in near:
        text_copies[1, dx, 0].start()
    text_copies[1, 0, 1].start()
    for dh in range(NH):
        for dx in near:
            text_copies[dh, dx, 0].wait_recv()
            text_copies[dh, dx, 1].start()
    for dh in range(NH):
        for dx in range(NX):
            text_copies[dh, dx, 1].wait_recv()

    for copy in tag_copies:
        copy.wait_recv()
    wanted = unpack_row(tagrecv_ref[...], spreader).astype(jnp.int32) - 1

    back_copies = [
        remote(
            gsend_ref.at[pl.ds(CAP * o, CAP)], back_ref.at[pl.ds(CAP * o, CAP)], back_sems, o,
            peer(dz=-ORDER[o][0], dy=ORDER[o][1]),
        )
        for o in range(SELF)
    ]
    lback_copies = [
        remote(
            losssend_ref.at[o], lossback_ref.at[o], lback_sems, o, peer(dz=-ORDER[o][0], dy=ORDER[o][1])
        )
        for o in range(SELF)
    ]

    arrived = 0
    for g in range(GROUPS):
        rows = pl.ds(g * GROUP, GROUP)
        while arrived < SELF and arrived * CAP < (g + 1) * GROUP:
            img_copies[arrived].wait_recv()
            arrived += 1
        wide = recv_ref[rows, :].astype(F32)
        inv = lax.rsqrt(jnp.sum(wide * wide, axis=1, keepdims=True) + EPS)
        inv_ref[...] = inv
        unit_ref[...] = (wide * inv).astype(BF16)
        isum_ref[...] = jnp.zeros_like(isum_ref)
        lsum_ref[...] = jnp.zeros_like(lsum_ref)
        hit = wanted[:, g * GROUP : (g + 1) * GROUP]

        def turn(t, carry, g=g, hit=hit):
            part = pl.ds(pl.multiple_of(t * TILE, TILE), TILE)
            block = texts_ref[part, :]
            unit = unit_ref[...]
            logit = temper * dot(block, unit, (1, 1)) + offset
            text = lax.broadcasted_iota(jnp.int32, logit.shape, 0) + t * TILE
            positive = text == hit
            m = jnp.where(positive, -logit, logit)
            e = jnp.exp(-jnp.abs(m))
            one = 1.0 + e
            series = e * (1.0 - e * (0.5 - e * (1.0 / 3.0)))
            log1p = jnp.where(e < 0.015625, series, jnp.log(one))
            lsum_ref[...] += jnp.sum(jnp.maximum(m, 0.0) + log1p, axis=0, keepdims=True)
            sigmoid = jnp.where(m >= 0.0, 1.0, e) / one
            coef = (jnp.where(positive, -temper, temper) * sigmoid).astype(BF16)
            text_part = dot(coef, unit, (1, 0))
            if g == 0:
                tsum_ref[part, :] = text_part
            else:
                tsum_ref[part, :] += text_part
            isum_ref[...] += dot(coef, block, (0, 0))
            return carry

        lax.fori_loop(0, TILES, turn, 0)

        image_sum = isum_ref[...]
        inv = inv_ref[...]
        unit = recv_ref[rows, :].astype(F32) * inv
        along = jnp.sum(unit * image_sum, axis=1, keepdims=True)
        gsend_ref[rows, :] = (inv * (image_sum - unit * along)).astype(BF16)
        row = (lsum_ref[...] / TEXTS).astype(BF16).astype(F32)
        parts = [jnp.zeros((1, GROUP), F32)] * GROUPS
        parts[g] = row
        if g == 0:
            losses = jnp.concatenate(parts, axis=1)
        else:
            losses = losses + jnp.concatenate(parts, axis=1)
        done = [o for o in range(BUCKETS) if g * GROUP < (o + 1) * CAP <= (g + 1) * GROUP]
        tiles = pack_row(losses, spreader)
        losssend_ref[pl.ds(done[0], len(done))] = tiles[done[0] : done[-1] + 1]
        for o in done:
            if o != SELF:
                back_copies[o].start()
                lback_copies[o].start()
    back_ref[kept, :] = gsend_ref[kept, :]
    lossback_ref[SELF] = losssend_ref[SELF]

    def block(ref, dh, dx, dc):
        return ref[pl.ds(ROWS * block_index(dh, dx, dc), ROWS), :]

    def pair(dh, dx):
        return dh * NX + dx

    far = (1, 3, 2, 0)
    sib_copies = {}
    for dh in (1, 0):
        for dx in far:
            k = pair(dh, dx)
            sibsend_ref[k] = block(tsum_ref, dh, dx, 1).astype(BF16)
            sib_copies[k] = remote(sibsend_ref.at[k], sibrecv_ref.at[k], sib_sems, k, peer(dc=1))
            sib_copies[k].start()
    x_copies = {}
    for dh in (1, 0):
        for dx in far:
            k = pair(dh, dx)
            sib_copies[k].wait_recv()
            total = block(tsum_ref, dh, dx, 0) + sibrecv_ref[k].astype(F32)
            if dx == 0:
                tsum_ref[pl.ds(ROWS * block_index(dh, 0, 0), ROWS), :] = total
            else:
                xsend_ref[k] = total.astype(BF16)
                x_copies[k] = remote(xsend_ref.at[k], xrecv_ref.at[k], x_sems, k, peer(dx=dx))
                x_copies[k].start()

    def gathered(dh):
        total = block(tsum_ref, dh, 0, 0)
        for dx in (1, 3, 2):
            x_copies[pair(dh, dx)].wait_recv()
            total = total + xrecv_ref[pair(dh, dx)].astype(F32)
        return total

    ysend_ref[...] = gathered(1).astype(BF16)
    y_copy = remote(ysend_ref, yrecv_ref, y_sems, 0, peer(dh=1))
    y_copy.start()
    total = gathered(0)
    y_copy.wait_recv()
    total = total + yrecv_ref[...].astype(F32)
    wide = txt_ref[...].astype(F32)
    inv = lax.rsqrt(jnp.sum(wide * wide, axis=1, keepdims=True) + EPS)
    unit = wide * inv
    along = jnp.sum(unit * total, axis=1, keepdims=True)
    tgrad_ref[...] = (inv * (total - unit * along)).astype(BF16)

    for o in range(SELF):
        back_copies[o].wait_recv()
        lback_copies[o].wait_recv()
    grad_ref[...] = dot(pick_ref[...], back_ref[...], (0, 0)).astype(BF16)
    row = unpack_row(lossback_ref[...], spreader)
    loss_ref[...] = dot(jnp.broadcast_to(row, (8, SLOTS)).astype(BF16), pick_ref[...], (1, 0))[0:1]

    for copies in (img_copies, tag_copies, back_copies, lback_copies):
        for copy in copies:
            copy.wait_send()
    for copies in (text_copies, sib_copies, x_copies):
        for copy in copies.values():
            copy.wait_send()
    y_copy.wait_send()


def body(images, texts, owners, labels, counts, scale, bias):
    vmem = pl.BlockSpec(memory_space=pltpu.VMEM)
    smem = pl.BlockSpec(memory_space=pltpu.SMEM)
    dma = pltpu.SemaphoreType.DMA
    block_rows = (ROWS, WIDTH)
    grads, loss, text_grads = pl.pallas_call(
        kernel,
        out_shape=(
            jax.ShapeDtypeStruct((PACK, WIDTH), BF16),
            jax.ShapeDtypeStruct((1, PACK), F32),
            jax.ShapeDtypeStruct(block_rows, BF16),
        ),
        in_specs=[vmem] * 4 + [smem] * 3,
        out_specs=(vmem, vmem, vmem),
        scratch_shapes=[
            pltpu.VMEM((SLOTS, PACK), BF16),
            pltpu.VMEM((SLOTS, WIDTH), BF16),
            pltpu.VMEM((SLOTS, WIDTH), BF16),
            pltpu.VMEM((GROUP, WIDTH), BF16),
            pltpu.VMEM((SLOTS, WIDTH), BF16),
            pltpu.VMEM((SLOTS, WIDTH), BF16),
            pltpu.VMEM((BUCKETS, 8, 128), F32),
            pltpu.VMEM((BUCKETS, 8, 128), F32),
            pltpu.VMEM((BUCKETS, 8, 128), F32),
            pltpu.VMEM((BUCKETS, 8, 128), F32),
            pltpu.VMEM((TEXTS, WIDTH), BF16),
            pltpu.VMEM((TEXTS, WIDTH), F32),
            pltpu.VMEM((GROUP, WIDTH), F32),
            pltpu.VMEM((1, GROUP), F32),
            pltpu.VMEM((GROUP, 1), F32),
            pltpu.VMEM((NH * NX,) + block_rows, BF16),
            pltpu.VMEM((NH * NX,) + block_rows, BF16),
            pltpu.VMEM((NH * NX,) + block_rows, BF16),
            pltpu.VMEM((NH * NX,) + block_rows, BF16),
            pltpu.VMEM(block_rows, BF16),
            pltpu.VMEM(block_rows, BF16),
            dma((2, SELF)),
            dma((2, SELF)),
            dma((2, SELF)),
            dma((2, SELF)),
            dma((2, BUCKETS)),
            dma((2, NH * NX)),
            dma((2, NH * NX)),
            dma((2, 1)),
        ],
        compiler_params=pltpu.CompilerParams(
            collective_id=0, has_side_effects=True, vmem_limit_bytes=56 << 20
        ),
    )(images, texts, owners.reshape(1, PACK), labels.reshape(1, PACK), counts, scale, bias)
    return grads, loss.reshape(PACK).astype(BF16), text_grads


def solution(mesh):
    rows = P(("dp", "blk"), None)
    line = P(("dp", "blk"))
    return jax.shard_map(
        body,
        mesh=mesh,
        in_specs=(rows, rows, rows, line, line, P(), P()),
        out_specs=(rows, line, rows),
        check_vma=False,
    )
```

```python
import functools

import jax
import jax.numpy as jnp
from jax import lax
from jax.experimental import pallas as pl
from jax.experimental.pallas import tpu as pltpu
from jax.sharding import PartitionSpec as P

MESH = pl.DeviceIdType.MESH
BF16 = jnp.bfloat16
F32 = jnp.float32
EPS = 1e-06

NZ, NY, NH, NX = 8, 2, 2, 4
PACK = 384
ROWS = 128
CAP = 48
BUCKETS = 16
SLOTS = CAP * BUCKETS
WIDTH = 1152
TEXTS = 2048
GROUP = 256
GROUPS = SLOTS // GROUP
HALF = ROWS // 2
COLUMNS = 1152

ORDER = (
    (0, 0), (0, 1), (1, 0), (7, 0), (1, 1), (7, 1),
    (2, 0), (6, 0), (2, 1), (6, 1), (3, 0),
    (5, 0), (3, 1), (5, 1), (4, 0), (4, 1),
)
SENT = range(1, BUCKETS)
EARLY = 10
DRAINED = 5


def place_of():
    p, c = lax.axis_index("dp"), lax.axis_index("blk")
    return p // NY, p % NY, c // (2 * NX), (c // 2) % NX, c % 2


def peer(dz=0, dy=0, dh=0, dx=0, dc=0):
    z, y, h, x, core = place_of()
    return (
        ((z + dz) % NZ) * NY + (y + dy) % NY,
        (((h + dh) % NH) * NX + (x + dx) % NX) * 2 + (core + dc) % 2,
    )


def block_index(dh, dx, dc):
    return (dh * 2 + dc) * NX + dx


def dot(a, b, dims):
    return lax.dot_general(a, b, ((dims[:1], dims[1:]), ((), ())), preferred_element_type=F32)


def spread():
    lane = lax.broadcasted_iota(jnp.int32, (128, SLOTS), 1)
    row = lax.broadcasted_iota(jnp.int32, (128, SLOTS), 0)
    return jnp.where(lane % CAP == row, 1.0, 0.0).astype(BF16)


def own_lanes(every):
    lane = lax.broadcasted_iota(jnp.int32, (128, SLOTS), 1)
    row = lax.broadcasted_iota(jnp.int32, (128, SLOTS), 0)
    own = lane // CAP == row // 8
    return own if every else own & (row % 8 == 0)


def pack_row(row, spreader):
    kept = jnp.where(own_lanes(True), row, 0.0).astype(BF16)
    return dot(kept, spreader, (1, 1)).reshape(BUCKETS, 8, 128)


def unpack_row(tiles, spreader):
    wide = dot(tiles.reshape(128, 128).astype(BF16), spreader, (1, 0))
    return jnp.sum(jnp.where(own_lanes(False), wide, 0.0), axis=0, keepdims=True)


def kernel(
    img_hbm, txt_hbm, own_ref, lab_ref, cnt_ref, scale_ref, bias_ref,
    back_ref, pick_hbm, loss_ref, tgrad_ref,
    img_ref, txt_ref, pick_ref, pick_t_ref, out_ref, recv_ref, unit_ref, coef_ref, gsend_ref,
    tagsend_ref, tagrecv_ref, losssend_ref, lossback_ref,
    texts_ref, tsum_ref, isum_ref,
    sibsend_ref, sibrecv_ref, xsend_ref, xrecv_ref, ysend_ref, yrecv_ref,
    img_sems, tag_sems, back_sems, lback_sems, txt_sems, sib_sems, x_sems, y_sems, local_sems,
):
    temper, offset, live_rows = scale_ref[0], bias_ref[0], cnt_ref[0]

    barrier = pltpu.get_barrier_semaphore()
    greeted = [peer(dz=ORDER[o][0], dy=ORDER[o][1]) for o in SENT]
    greeted += [peer(dc=1), peer(dh=1), peer(dx=1), peer(dx=3)]
    for device in greeted:
        pl.semaphore_signal(barrier, inc=1, device_id=device, device_id_type=MESH)
    img_load = pltpu.make_async_copy(img_hbm, img_ref, local_sems.at[0])
    txt_load = pltpu.make_async_copy(txt_hbm, txt_ref, local_sems.at[1])
    img_load.start()
    txt_load.start()

    def remote(src, dst, sems, index, device):
        return pltpu.make_async_remote_copy(
            src_ref=src,
            dst_ref=dst,
            send_sem=sems.at[0, index],
            recv_sem=sems.at[1, index],
            device_id=device,
            device_id_type=MESH,
        )

    bucket = lax.broadcasted_iota(jnp.int32, (BUCKETS, PACK), 0)
    owner_of = jnp.zeros((BUCKETS, PACK), jnp.int32)
    for o, (dz, dy) in enumerate(ORDER):
        owner_of = jnp.where(bucket == o, peer(dz=dz, dy=dy)[0], owner_of)
    live = lax.broadcasted_iota(jnp.int32, (BUCKETS, PACK), 1) < live_rows
    onehot = jnp.where((own_ref[...] == owner_of) & live, 1.0, 0.0)
    earlier = jnp.where(
        lax.broadcasted_iota(jnp.int32, (PACK, PACK), 0)
        < lax.broadcasted_iota(jnp.int32, (PACK, PACK), 1),
        1.0,
        0.0,
    ).astype(BF16)
    before = dot(onehot.astype(BF16), earlier, (1, 0))
    target = jnp.sum(onehot * (before + (bucket * CAP + 1).astype(F32)), axis=0, keepdims=True)
    target = target.astype(jnp.int32) - 1
    slot = lax.broadcasted_iota(jnp.int32, (SLOTS, PACK), 0)
    pick_ref[...] = jnp.where(slot == target, 1.0, 0.0).astype(BF16)
    spreader = spread()
    tags = dot(
        jnp.broadcast_to((lab_ref[...].reshape(1, PACK) + 1).astype(F32), (8, PACK)).astype(BF16),
        pick_ref[...],
        (1, 1),
    )
    tagsend_ref[...] = pack_row(tags[0:1], spreader)
    tagrecv_ref[0] = tagsend_ref[0]

    def bucket_rows(o):
        return pl.ds(CAP * o, CAP)

    def away(o):
        return peer(dz=ORDER[o][0], dy=ORDER[o][1])

    def home(o):
        return peer(dz=-ORDER[o][0], dy=ORDER[o][1])

    img_copies, tag_copies, back_copies, lback_copies = {}, {}, {}, {}
    for o in SENT:
        rows = bucket_rows(o)
        img_copies[o] = remote(out_ref.at[rows], recv_ref.at[rows], img_sems, o, away(o))
        tag_copies[o] = remote(tagsend_ref.at[o], tagrecv_ref.at[o], tag_sems, o, away(o))
        back_copies[o] = remote(gsend_ref.at[rows], back_ref.at[rows], back_sems, o, home(o))
        lback_copies[o] = remote(losssend_ref.at[o], lossback_ref.at[o], lback_sems, o, home(o))

    img_load.wait()
    out_ref[...] = dot(pick_ref[...], img_ref[...], (1, 0)).astype(BF16)
    txt_load.wait()
    wide = txt_ref[...].astype(F32)
    texts_ref[pl.ds(0, ROWS), :] = (
        wide * lax.rsqrt(jnp.sum(wide * wide, axis=1, keepdims=True) + EPS)
    ).astype(BF16)
    pl.semaphore_wait(barrier, len(greeted))
    for o in SENT[:EARLY]:
        img_copies[o].start()

    def text_rows(dh, dx, dc, first=0, count=ROWS):
        return texts_ref.at[pl.ds(ROWS * block_index(dh, dx, dc) + first, count)]

    text_copies = {}

    def text_send(key, src, dst, device):
        text_copies[key] = remote(src, dst, txt_sems, len(text_copies), device)
        text_copies[key].start()

    def to_sibling(dh, dx):
        text_send(("c", dh, dx), text_rows(dh, dx, 0), text_rows(dh, dx, 1), peer(dc=1))

    def to_neighbours(dh):
        text_send(("x", dh, 3), text_rows(dh, 0, 0), text_rows(dh, 3, 0), peer(dx=1))
        text_send(("x", dh, 1), text_rows(dh, 0, 0), text_rows(dh, 1, 0), peer(dx=3))

    def relay(dh):
        text_copies["x", dh, 3].wait_recv()
        text_send(("r", dh, 0), text_rows(dh, 3, 0, 0, HALF), text_rows(dh, 2, 0, 0, HALF), peer(dx=1))
        to_sibling(dh, 3)
        text_copies["x", dh, 1].wait_recv()
        text_send(
            ("r", dh, 1), text_rows(dh, 1, 0, HALF, HALF), text_rows(dh, 2, 0, HALF, HALF), peer(dx=3)
        )
        to_sibling(dh, 1)

    def relayed(dh):
        text_copies["r", dh, 0].wait_recv()
        text_copies["r", dh, 1].wait_recv()
        to_sibling(dh, 2)

    text_send("h", text_rows(0, 0, 0), text_rows(1, 0, 0), peer(dh=1))
    to_neighbours(0)
    to_sibling(0, 0)
    for o in SENT:
        tag_copies[o].start()
    recv_ref[bucket_rows(0), :] = out_ref[bucket_rows(0), :]
    pick_t_ref[...] = pick_ref[...].T
    pick_save = pltpu.make_async_copy(pick_t_ref, pick_hbm, local_sems.at[0])
    pick_save.start()
    inv, loss_sum, hits, sib_copies = {}, {}, {}, {}
    far = (2, 1, 3, 0)

    def group_rows(g):
        return pl.ds(g * GROUP, GROUP)

    def prepare(g, first, end):
        for o in range(max(first, 1), end):
            img_copies[o].wait_recv()
        wide = recv_ref[group_rows(g), :].astype(F32)
        inv[g] = lax.rsqrt(jnp.sum(wide * wide, axis=1, keepdims=True) + EPS)
        unit_ref[group_rows(g), :] = (wide * inv[g]).astype(BF16)

    def weigh(g, dh):
        half = pl.ds(dh * TEXTS // 2, TEXTS // 2)
        logit = temper * dot(texts_ref[half, :], unit_ref[group_rows(g), :], (1, 1)) + offset
        text = lax.broadcasted_iota(jnp.int32, logit.shape, 0) + dh * TEXTS // 2
        positive = text == hits["all"][:, g * GROUP : (g + 1) * GROUP]
        m = jnp.where(positive, -logit, logit)
        e = jnp.exp(-jnp.abs(m))
        one = 1.0 + e
        series = e * (1.0 - e * (0.5 - e * (1.0 / 3.0)))
        log1p = jnp.where(e < 0.015625, series, jnp.log(one))
        part_sum = jnp.sum(jnp.maximum(m, 0.0) + log1p, axis=0, keepdims=True)
        loss_sum[g] = loss_sum[g] + part_sum if g in loss_sum else part_sum
        sigmoid = jnp.where(m >= 0.0, 1.0, e) / one
        coef_ref[...] = (jnp.where(positive, -temper, temper) * sigmoid).astype(BF16)
        for dc in (1, 0):
            own = pl.ds(dc * TEXTS // 4, TEXTS // 4)
            part = pl.ds((dh * 2 + dc) * TEXTS // 4, TEXTS // 4)
            text_part = dot(coef_ref[own, :], unit_ref[group_rows(g), :], (1, 0))
            if g == 0:
                tsum_ref[part, :] = text_part
            else:
                tsum_ref[part, :] += text_part
            if g == GROUPS - 1 and dc:
                for dx in far:
                    k = dh * NX + dx
                    sibsend_ref[k] = tsum_ref[pl.ds(ROWS * block_index(dh, dx, 1), ROWS), :].astype(BF16)
                    sib_copies[k] = remote(sibsend_ref.at[k], sibrecv_ref.at[k], sib_sems, k, peer(dc=1))
                    sib_copies[k].start()
        image_part = dot(coef_ref[...], texts_ref[half, :], (0, 0))
        if dh == (1 if g == GROUPS - 1 else 0):
            isum_ref[group_rows(g), :] = image_part
        else:
            isum_ref[group_rows(g), :] += image_part

    def project(g):
        image_sum = isum_ref[group_rows(g), :]
        unit = recv_ref[group_rows(g), :].astype(F32) * inv[g]
        along = jnp.sum(unit * image_sum, axis=1, keepdims=True)
        gsend_ref[group_rows(g), :] = (inv[g] * (image_sum - unit * along)).astype(BF16)

    def complete(dh):
        for dx in range(NX):
            text_copies["c", dh, dx].wait_recv()

    relay(0)
    text_copies["h"].wait_recv()
    to_neighbours(1)
    to_sibling(1, 0)
    for o in SENT[:DRAINED]:
        img_copies[o].wait_send()
    for o in SENT[EARLY:]:
        img_copies[o].start()
    relayed(0)
    for o in SENT:
        tag_copies[o].wait_recv()
    hits["all"] = unpack_row(tagrecv_ref[...], spreader).astype(jnp.int32) - 1
    complete(0)
    prepare(0, 0, 6)
    weigh(0, 0)
    relay(1)
    prepare(1, 6, 11)
    weigh(1, 0)
    relayed(1)
    complete(1)
    weigh(0, 1)
    project(0)
    for o in range(1, 5):
        back_copies[o].start()
    weigh(1, 1)
    project(1)
    for o in range(5, 10):
        back_copies[o].start()
    prepare(2, 11, BUCKETS)
    weigh(2, 1)
    weigh(2, 0)
    project(2)
    for o in range(10, BUCKETS):
        back_copies[o].start()
    losses = jnp.concatenate([loss_sum[g] for g in range(GROUPS)], axis=1)
    losses = (losses / TEXTS).astype(BF16).astype(F32)
    losssend_ref[...] = pack_row(losses, spreader)
    keep = pltpu.make_async_copy(
        gsend_ref.at[bucket_rows(0)], back_ref.at[bucket_rows(0)], local_sems.at[1]
    )
    keep.start()
    for o in SENT:
        lback_copies[o].start()
    lossback_ref[0] = losssend_ref[0]

    x_copies = {}

    def x_send(dh, m, value):
        xsend_ref[dh, m] = value.astype(BF16)
        device = peer(dx=3 if m % 2 else 1)
        x_copies[dh, m] = remote(xsend_ref.at[dh, m], xrecv_ref.at[dh, m], x_sems, dh * 6 + m, device)
        x_copies[dh, m].start()

    def x_received(dh, m):
        x_copies[dh, m].wait_recv()
        return xrecv_ref[dh, m].astype(F32)

    def chip_sum(dh, dx):
        k = dh * NX + dx
        sib_copies[k].wait_recv()
        total = tsum_ref[pl.ds(ROWS * block_index(dh, dx, 0), ROWS), :] + sibrecv_ref[k].astype(F32)
        return total[:HALF], total[HALF:]

    kept = {}
    for dh in (1, 0):
        low, high = chip_sum(dh, 2)
        x_send(dh, 0, low)
        x_send(dh, 1, high)
        ahead, high = chip_sum(dh, 1)
        x_send(dh, 2, high)
        low, behind = chip_sum(dh, 3)
        x_send(dh, 3, low)
        kept[dh] = chip_sum(dh, 0)
        x_send(dh, 4, ahead + x_received(dh, 0))
        x_send(dh, 5, behind + x_received(dh, 1))

    def gathered(dh):
        low, high = kept[dh]
        return jnp.concatenate(
            [
                low + x_received(dh, 3) + x_received(dh, 4),
                high + x_received(dh, 2) + x_received(dh, 5),
            ],
            axis=0,
        )

    ysend_ref[...] = gathered(1).astype(BF16)
    y_copy = remote(ysend_ref, yrecv_ref, y_sems, 0, peer(dh=1))
    y_copy.start()
    total = gathered(0)
    y_copy.wait_recv()
    total = total + yrecv_ref[...].astype(F32)
    wide = txt_ref[...].astype(F32)
    inv = lax.rsqrt(jnp.sum(wide * wide, axis=1, keepdims=True) + EPS)
    unit = wide * inv
    along = jnp.sum(unit * total, axis=1, keepdims=True)
    tgrad_ref[...] = (inv * (total - unit * along)).astype(BF16)

    pick_save.wait()
    keep.wait()
    y_copy.wait_send()
    for o in SENT[DRAINED:]:
        img_copies[o].wait_send()
    for copies in (text_copies, tag_copies, sib_copies, x_copies):
        for copy in copies.values():
            copy.wait_send()
    for copy in lback_copies.values():
        copy.wait()
    row = jnp.broadcast_to(unpack_row(lossback_ref[...], spreader), (8, SLOTS)).astype(BF16)
    loss_ref[...] = dot(row, pick_ref[...], (1, 0))[0:1]
    for copy in back_copies.values():
        copy.wait()


def finish(back_ref, pick_ref, losses_ref, sums_ref, grad_ref, loss_ref, tgrad_ref):
    grad_ref[...] = dot(pick_ref[...], back_ref[...], (1, 0)).astype(BF16)
    tgrad_ref[...] = sums_ref[...]
    loss_ref[...] = losses_ref[...].astype(BF16).reshape(PACK)


def body(images, texts, owners, labels, counts, scale, bias):
    vmem = pl.BlockSpec(memory_space=pltpu.VMEM)
    smem = pl.BlockSpec(memory_space=pltpu.SMEM)
    anywhere = pl.BlockSpec(memory_space=pl.ANY)
    dma = pltpu.SemaphoreType.DMA
    blocks = NH * NX
    back, pick, losses, sums = pl.pallas_call(
        kernel,
        out_shape=(
            jax.ShapeDtypeStruct((SLOTS, WIDTH), BF16),
            jax.ShapeDtypeStruct((PACK, SLOTS), BF16),
            jax.ShapeDtypeStruct((1, PACK), F32),
            jax.ShapeDtypeStruct((ROWS, WIDTH), BF16),
        ),
        in_specs=[anywhere] * 2 + [vmem] * 2 + [smem] * 3,
        out_specs=(anywhere, anywhere, vmem, vmem),
        scratch_shapes=[
            pltpu.VMEM((PACK, WIDTH), BF16),
            pltpu.VMEM((ROWS, WIDTH), BF16),
            pltpu.VMEM((SLOTS, PACK), BF16),
            pltpu.VMEM((PACK, SLOTS), BF16),
            pltpu.VMEM((SLOTS, WIDTH), BF16),
            pltpu.VMEM((SLOTS, WIDTH), BF16),
            pltpu.VMEM((SLOTS, WIDTH), BF16),
            pltpu.VMEM((TEXTS // 2, GROUP), BF16),
            pltpu.VMEM((SLOTS, WIDTH), BF16),
            pltpu.VMEM((BUCKETS, 8, 128), F32),
            pltpu.VMEM((BUCKETS, 8, 128), F32),
            pltpu.VMEM((BUCKETS, 8, 128), F32),
            pltpu.VMEM((BUCKETS, 8, 128), F32),
            pltpu.VMEM((TEXTS, WIDTH), BF16),
            pltpu.VMEM((TEXTS, WIDTH), F32),
            pltpu.VMEM((SLOTS, WIDTH), F32),
            pltpu.VMEM((blocks, ROWS, WIDTH), BF16),
            pltpu.VMEM((blocks, ROWS, WIDTH), BF16),
            pltpu.VMEM((NH, 6, HALF, WIDTH), BF16),
            pltpu.VMEM((NH, 6, HALF, WIDTH), BF16),
            pltpu.VMEM((ROWS, WIDTH), BF16),
            pltpu.VMEM((ROWS, WIDTH), BF16),
            dma((2, BUCKETS)),
            dma((2, BUCKETS)),
            dma((2, BUCKETS)),
            dma((2, BUCKETS)),
            dma((2, 17)),
            dma((2, blocks)),
            dma((2, 6 * NH)),
            dma((2, 1)),
            dma((2,)),
        ],
        compiler_params=pltpu.CompilerParams(
            collective_id=0, has_side_effects=True, vmem_limit_bytes=56 << 20
        ),
    )(images, texts, owners.reshape(1, PACK), labels, counts, scale, bias)
    columns = lambda rows: pl.BlockSpec((rows, COLUMNS), lambda i: (0, i))
    grads, loss, text_grads = pl.pallas_call(
        finish,
        grid=(WIDTH // COLUMNS,),
        out_shape=(
            jax.ShapeDtypeStruct((PACK, WIDTH), BF16),
            jax.ShapeDtypeStruct((PACK,), BF16),
            jax.ShapeDtypeStruct((ROWS, WIDTH), BF16),
        ),
        in_specs=[
            columns(SLOTS),
            pl.BlockSpec((PACK, SLOTS), lambda i: (0, 0)),
            pl.BlockSpec((1, PACK), lambda i: (0, 0)),
            columns(ROWS),
        ],
        out_specs=(columns(PACK), pl.BlockSpec((PACK,), lambda i: (0,)), columns(ROWS)),
        compiler_params=pltpu.CompilerParams(vmem_limit_bytes=60 << 20),
    )(back, pick, losses, sums)
    return grads, loss, text_grads


def solution(mesh):
    rows = P(("dp", "blk"), None)
    line = P(("dp", "blk"))
    return jax.shard_map(
        body,
        mesh=mesh,
        in_specs=(rows, rows, rows, line, line, P(), P()),
        out_specs=(rows, line, rows),
        check_vma=False,
    )
```

```python
import functools

import jax
import jax.numpy as jnp
from jax import lax
from jax.experimental import pallas as pl
from jax.experimental.pallas import tpu as pltpu
from jax.sharding import PartitionSpec as P

MESH = pl.DeviceIdType.MESH
BF16 = jnp.bfloat16
F32 = jnp.float32
EPS = 1e-06

NZ, NY, NH, NX = 8, 2, 2, 4
PACK = 384
ROWS = 128
CAP = 48
BUCKETS = 16
SLOTS = CAP * BUCKETS
WIDTH = 1152
TEXTS = 2048
GROUP = 256
GROUPS = SLOTS // GROUP
HALF = ROWS // 2
COLUMNS = 1152

ORDER = (
    (0, 0), (0, 1), (1, 0), (7, 0), (1, 1), (7, 1),
    (2, 0), (6, 0), (2, 1), (6, 1), (3, 0),
    (5, 0), (3, 1), (5, 1), (4, 0), (4, 1),
)
SENT = range(1, BUCKETS)
BATCHES = (SENT[:7], SENT[7:11], SENT[11:])
LEFT = (SENT[:4], SENT[4:7], SENT[7:])


def place_of():
    p, c = lax.axis_index("dp"), lax.axis_index("blk")
    return p // NY, p % NY, c // (2 * NX), (c // 2) % NX, c % 2


def peer(dz=0, dy=0, dh=0, dx=0, dc=0):
    z, y, h, x, core = place_of()
    return (
        ((z + dz) % NZ) * NY + (y + dy) % NY,
        (((h + dh) % NH) * NX + (x + dx) % NX) * 2 + (core + dc) % 2,
    )


def block_index(dh, dx, dc):
    return (dh * 2 + dc) * NX + dx


def dot(a, b, dims):
    return lax.dot_general(a, b, ((dims[:1], dims[1:]), ((), ())), preferred_element_type=F32)


def spread():
    lane = lax.broadcasted_iota(jnp.int32, (128, SLOTS), 1)
    row = lax.broadcasted_iota(jnp.int32, (128, SLOTS), 0)
    return jnp.where(lane % CAP == row, 1.0, 0.0).astype(BF16)


def own_lanes(every):
    lane = lax.broadcasted_iota(jnp.int32, (128, SLOTS), 1)
    row = lax.broadcasted_iota(jnp.int32, (128, SLOTS), 0)
    own = lane // CAP == row // 8
    return own if every else own & (row % 8 == 0)


def pack_row(row, spreader):
    kept = jnp.where(own_lanes(True), row, 0.0).astype(BF16)
    return dot(kept, spreader, (1, 1)).reshape(BUCKETS, 8, 128)


def unpack_row(tiles, spreader):
    wide = dot(tiles.reshape(128, 128).astype(BF16), spreader, (1, 0))
    return jnp.sum(jnp.where(own_lanes(False), wide, 0.0), axis=0, keepdims=True)


def kernel(
    img_hbm, txt_hbm, own_ref, lab_ref, cnt_ref, scale_ref, bias_ref,
    back_ref, pick_hbm, loss_ref, tgrad_ref,
    img_ref, txt_ref, pick_ref, pick_t_ref, out_ref, recv_ref, unit_ref, coef_ref, gsend_ref,
    tagsend_ref, tagrecv_ref, losssend_ref, lossback_ref,
    texts_ref, tsum_ref, isum_ref,
    sibsend_ref, sibrecv_ref, xsend_ref, xrecv_ref, ysend_ref, yrecv_ref,
    img_sems, tag_sems, back_sems, lback_sems, txt_sems, sib_sems, x_sems, y_sems, local_sems,
):
    temper, offset, live_rows = scale_ref[0], bias_ref[0], cnt_ref[0]

    barrier = pltpu.get_barrier_semaphore()
    greeted = [peer(dz=ORDER[o][0], dy=ORDER[o][1]) for o in SENT]
    greeted += [peer(dc=1), peer(dh=1), peer(dx=1), peer(dx=3)]
    for device in greeted:
        pl.semaphore_signal(barrier, inc=1, device_id=device, device_id_type=MESH)
    img_load = pltpu.make_async_copy(img_hbm, img_ref, local_sems.at[0])
    txt_load = pltpu.make_async_copy(txt_hbm, txt_ref, local_sems.at[1])
    img_load.start()
    txt_load.start()

    def remote(src, dst, sems, index, device):
        return pltpu.make_async_remote_copy(
            src_ref=src,
            dst_ref=dst,
            send_sem=sems.at[0, index],
            recv_sem=sems.at[1, index],
            device_id=device,
            device_id_type=MESH,
        )

    bucket = lax.broadcasted_iota(jnp.int32, (BUCKETS, PACK), 0)
    owner_of = jnp.zeros((BUCKETS, PACK), jnp.int32)
    for o, (dz, dy) in enumerate(ORDER):
        owner_of = jnp.where(bucket == o, peer(dz=dz, dy=dy)[0], owner_of)
    live = lax.broadcasted_iota(jnp.int32, (BUCKETS, PACK), 1) < live_rows
    onehot = jnp.where((own_ref[...] == owner_of) & live, 1.0, 0.0)
    earlier = jnp.where(
        lax.broadcasted_iota(jnp.int32, (PACK, PACK), 0)
        < lax.broadcasted_iota(jnp.int32, (PACK, PACK), 1),
        1.0,
        0.0,
    ).astype(BF16)
    before = dot(onehot.astype(BF16), earlier, (1, 0))
    target = jnp.sum(onehot * (before + (bucket * CAP + 1).astype(F32)), axis=0, keepdims=True)
    target = target.astype(jnp.int32) - 1
    slot = lax.broadcasted_iota(jnp.int32, (SLOTS, PACK), 0)
    pick_ref[...] = jnp.where(slot == target, 1.0, 0.0).astype(BF16)
    spreader = spread()
    tags = dot(
        jnp.broadcast_to((lab_ref[...].reshape(1, PACK) + 1).astype(F32), (8, PACK)).astype(BF16),
        pick_ref[...],
        (1, 1),
    )
    tagsend_ref[...] = pack_row(tags[0:1], spreader)
    tagrecv_ref[0] = tagsend_ref[0]

    def bucket_rows(o):
        return pl.ds(CAP * o, CAP)

    def away(o):
        return peer(dz=ORDER[o][0], dy=ORDER[o][1])

    def home(o):
        return peer(dz=-ORDER[o][0], dy=ORDER[o][1])

    img_copies, tag_copies, back_copies, lback_copies = {}, {}, {}, {}
    for o in SENT:
        rows = bucket_rows(o)
        img_copies[o] = remote(out_ref.at[rows], recv_ref.at[rows], img_sems, o, away(o))
        tag_copies[o] = remote(tagsend_ref.at[o], tagrecv_ref.at[o], tag_sems, o, away(o))
        back_copies[o] = remote(gsend_ref.at[rows], back_ref.at[rows], back_sems, o, home(o))
        lback_copies[o] = remote(losssend_ref.at[o], lossback_ref.at[o], lback_sems, o, home(o))

    img_load.wait()
    out_ref[...] = dot(pick_ref[...], img_ref[...], (1, 0)).astype(BF16)
    txt_load.wait()
    wide = txt_ref[...].astype(F32)
    texts_ref[pl.ds(0, ROWS), :] = (
        wide * lax.rsqrt(jnp.sum(wide * wide, axis=1, keepdims=True) + EPS)
    ).astype(BF16)
    pl.semaphore_wait(barrier, len(greeted))
    for o in SENT:
        tag_copies[o].start()
    for o in BATCHES[0]:
        img_copies[o].start()

    def text_rows(dh, dx, dc, first=0, count=ROWS):
        return texts_ref.at[pl.ds(ROWS * block_index(dh, dx, dc) + first, count)]

    text_copies = {}

    def text_send(key, src, dst, device):
        text_copies[key] = remote(src, dst, txt_sems, len(text_copies), device)
        text_copies[key].start()

    def to_sibling(dh, dx):
        text_send(("c", dh, dx), text_rows(dh, dx, 0), text_rows(dh, dx, 1), peer(dc=1))

    def to_neighbours(dh):
        text_send(("x", dh, 3), text_rows(dh, 0, 0), text_rows(dh, 3, 0), peer(dx=1))
        text_send(("x", dh, 1), text_rows(dh, 0, 0), text_rows(dh, 1, 0), peer(dx=3))

    def relay(dh):
        text_copies["x", dh, 3].wait_recv()
        text_send(("r", dh, 0), text_rows(dh, 3, 0, 0, HALF), text_rows(dh, 2, 0, 0, HALF), peer(dx=1))
        to_sibling(dh, 3)
        text_copies["x", dh, 1].wait_recv()
        text_send(
            ("r", dh, 1), text_rows(dh, 1, 0, HALF, HALF), text_rows(dh, 2, 0, HALF, HALF), peer(dx=3)
        )
        to_sibling(dh, 1)

    def relayed(dh):
        text_copies["r", dh, 0].wait_recv()
        text_copies["r", dh, 1].wait_recv()
        to_sibling(dh, 2)

    text_send("h", text_rows(0, 0, 0), text_rows(1, 0, 0), peer(dh=1))
    to_neighbours(0)
    to_sibling(0, 0)
    recv_ref[bucket_rows(0), :] = out_ref[bucket_rows(0), :]
    pick_t_ref[...] = pick_ref[...].T
    pick_save = pltpu.make_async_copy(pick_t_ref, pick_hbm, local_sems.at[0])
    pick_save.start()
    inv, loss_sum, hits, sib_copies = {}, {}, {}, {}
    far = (2, 1, 3, 0)

    def group_rows(g):
        return pl.ds(g * GROUP, GROUP)

    def prepare(g, first, end):
        for o in range(max(first, 1), end):
            img_copies[o].wait_recv()
        wide = recv_ref[group_rows(g), :].astype(F32)
        inv[g] = lax.rsqrt(jnp.sum(wide * wide, axis=1, keepdims=True) + EPS)
        unit_ref[group_rows(g), :] = (wide * inv[g]).astype(BF16)

    def weigh(g, dh):
        half = pl.ds(dh * TEXTS // 2, TEXTS // 2)
        logit = temper * dot(texts_ref[half, :], unit_ref[group_rows(g), :], (1, 1)) + offset
        text = lax.broadcasted_iota(jnp.int32, logit.shape, 0) + dh * TEXTS // 2
        positive = text == hits["all"][:, g * GROUP : (g + 1) * GROUP]
        m = jnp.where(positive, -logit, logit)
        e = jnp.exp(-jnp.abs(m))
        one = 1.0 + e
        series = e * (1.0 - e * (0.5 - e * (1.0 / 3.0)))
        log1p = jnp.where(e < 0.015625, series, jnp.log(one))
        part_sum = jnp.sum(jnp.maximum(m, 0.0) + log1p, axis=0, keepdims=True)
        loss_sum[g] = loss_sum[g] + part_sum if g in loss_sum else part_sum
        sigmoid = jnp.where(m >= 0.0, 1.0, e) / one
        coef_ref[...] = (jnp.where(positive, -temper, temper) * sigmoid).astype(BF16)
        for dc in (1, 0):
            own = pl.ds(dc * TEXTS // 4, TEXTS // 4)
            part = pl.ds((dh * 2 + dc) * TEXTS // 4, TEXTS // 4)
            text_part = dot(coef_ref[own, :], unit_ref[group_rows(g), :], (1, 0))
            if g == 0:
                tsum_ref[part, :] = text_part
            else:
                tsum_ref[part, :] += text_part
            if g == GROUPS - 1 and dc:
                for dx in far:
                    k = dh * NX + dx
                    sibsend_ref[k] = tsum_ref[pl.ds(ROWS * block_index(dh, dx, 1), ROWS), :].astype(BF16)
                    sib_copies[k] = remote(sibsend_ref.at[k], sibrecv_ref.at[k], sib_sems, k, peer(dc=1))
                    sib_copies[k].start()
        image_part = dot(coef_ref[...], texts_ref[half, :], (0, 0))
        if dh == (1 if g == GROUPS - 1 else 0):
            isum_ref[group_rows(g), :] = image_part
        else:
            isum_ref[group_rows(g), :] += image_part

    def project(g):
        image_sum = isum_ref[group_rows(g), :]
        unit = recv_ref[group_rows(g), :].astype(F32) * inv[g]
        along = jnp.sum(unit * image_sum, axis=1, keepdims=True)
        gsend_ref[group_rows(g), :] = (inv[g] * (image_sum - unit * along)).astype(BF16)

    def complete(dh):
        for dx in range(NX):
            text_copies["c", dh, dx].wait_recv()

    def next_batch(i):
        for o in LEFT[i]:
            img_copies[o].wait_send()
        for o in BATCHES[i + 1]:
            img_copies[o].start()

    next_batch(0)
    relay(0)
    text_copies["h"].wait_recv()
    to_neighbours(1)
    to_sibling(1, 0)
    relayed(0)
    for o in SENT:
        tag_copies[o].wait_recv()
    hits["all"] = unpack_row(tagrecv_ref[...], spreader).astype(jnp.int32) - 1
    complete(0)
    prepare(0, 0, 6)
    weigh(0, 0)
    next_batch(1)
    relay(1)
    prepare(1, 6, 11)
    weigh(1, 0)
    relayed(1)
    complete(1)
    weigh(0, 1)
    project(0)
    for o in range(1, 5):
        back_copies[o].start()
    weigh(1, 1)
    project(1)
    for o in range(5, 10):
        back_copies[o].start()
    prepare(2, 11, BUCKETS)
    weigh(2, 1)
    weigh(2, 0)
    losses = jnp.concatenate([loss_sum[g] for g in range(GROUPS)], axis=1)
    losses = (losses / TEXTS).astype(BF16).astype(F32)
    losssend_ref[...] = pack_row(losses, spreader)
    for o in SENT:
        lback_copies[o].start()
    lossback_ref[0] = losssend_ref[0]
    project(2)
    for o in range(10, BUCKETS):
        back_copies[o].start()
    keep = pltpu.make_async_copy(
        gsend_ref.at[bucket_rows(0)], back_ref.at[bucket_rows(0)], local_sems.at[1]
    )
    keep.start()

    x_copies = {}

    def x_send(dh, m, value):
        xsend_ref[dh, m] = value.astype(BF16)
        device = peer(dx=3 if m % 2 else 1)
        x_copies[dh, m] = remote(xsend_ref.at[dh, m], xrecv_ref.at[dh, m], x_sems, dh * 6 + m, device)
        x_copies[dh, m].start()

    def x_received(dh, m):
        x_copies[dh, m].wait_recv()
        return xrecv_ref[dh, m].astype(F32)

    def chip_sum(dh, dx):
        k = dh * NX + dx
        sib_copies[k].wait_recv()
        total = tsum_ref[pl.ds(ROWS * block_index(dh, dx, 0), ROWS), :] + sibrecv_ref[k].astype(F32)
        return total[:HALF], total[HALF:]

    kept = {}
    for dh in (1, 0):
        low, high = chip_sum(dh, 2)
        x_send(dh, 0, low)
        x_send(dh, 1, high)
        ahead, high = chip_sum(dh, 1)
        x_send(dh, 2, high)
        low, behind = chip_sum(dh, 3)
        x_send(dh, 3, low)
        kept[dh] = chip_sum(dh, 0)
        x_send(dh, 4, ahead + x_received(dh, 0))
        x_send(dh, 5, behind + x_received(dh, 1))

    def gathered(dh):
        low, high = kept[dh]
        return jnp.concatenate(
            [
                low + x_received(dh, 3) + x_received(dh, 4),
                high + x_received(dh, 2) + x_received(dh, 5),
            ],
            axis=0,
        )

    ysend_ref[...] = gathered(1).astype(BF16)
    y_copy = remote(ysend_ref, yrecv_ref, y_sems, 0, peer(dh=1))
    y_copy.start()
    total = gathered(0)
    y_copy.wait_recv()
    total = total + yrecv_ref[...].astype(F32)
    wide = txt_ref[...].astype(F32)
    inv = lax.rsqrt(jnp.sum(wide * wide, axis=1, keepdims=True) + EPS)
    unit = wide * inv
    along = jnp.sum(unit * total, axis=1, keepdims=True)
    tgrad_ref[...] = (inv * (total - unit * along)).astype(BF16)

    pick_save.wait()
    keep.wait()
    y_copy.wait_send()
    for o in LEFT[2]:
        img_copies[o].wait_send()
    for copies in (text_copies, tag_copies, sib_copies, x_copies):
        for copy in copies.values():
            copy.wait_send()
    for copy in lback_copies.values():
        copy.wait()
    row = jnp.broadcast_to(unpack_row(lossback_ref[...], spreader), (8, SLOTS)).astype(BF16)
    loss_ref[...] = dot(row, pick_ref[...], (1, 0))[0:1]
    for copy in back_copies.values():
        copy.wait()


def finish(back_ref, pick_ref, losses_ref, sums_ref, grad_ref, loss_ref, tgrad_ref):
    grad_ref[...] = dot(pick_ref[...], back_ref[...], (1, 0)).astype(BF16)
    tgrad_ref[...] = sums_ref[...]
    loss_ref[...] = losses_ref[...].astype(BF16).reshape(PACK)


def body(images, texts, owners, labels, counts, scale, bias):
    vmem = pl.BlockSpec(memory_space=pltpu.VMEM)
    smem = pl.BlockSpec(memory_space=pltpu.SMEM)
    anywhere = pl.BlockSpec(memory_space=pl.ANY)
    dma = pltpu.SemaphoreType.DMA
    blocks = NH * NX
    back, pick, losses, sums = pl.pallas_call(
        kernel,
        out_shape=(
            jax.ShapeDtypeStruct((SLOTS, WIDTH), BF16),
            jax.ShapeDtypeStruct((PACK, SLOTS), BF16),
            jax.ShapeDtypeStruct((1, PACK), F32),
            jax.ShapeDtypeStruct((ROWS, WIDTH), BF16),
        ),
        in_specs=[anywhere] * 2 + [vmem] * 2 + [smem] * 3,
        out_specs=(anywhere, anywhere, vmem, vmem),
        scratch_shapes=[
            pltpu.VMEM((PACK, WIDTH), BF16),
            pltpu.VMEM((ROWS, WIDTH), BF16),
            pltpu.VMEM((SLOTS, PACK), BF16),
            pltpu.VMEM((PACK, SLOTS), BF16),
            pltpu.VMEM((SLOTS, WIDTH), BF16),
            pltpu.VMEM((SLOTS, WIDTH), BF16),
            pltpu.VMEM((SLOTS, WIDTH), BF16),
            pltpu.VMEM((TEXTS // 2, GROUP), BF16),
            pltpu.VMEM((SLOTS, WIDTH), BF16),
            pltpu.VMEM((BUCKETS, 8, 128), F32),
            pltpu.VMEM((BUCKETS, 8, 128), F32),
            pltpu.VMEM((BUCKETS, 8, 128), F32),
            pltpu.VMEM((BUCKETS, 8, 128), F32),
            pltpu.VMEM((TEXTS, WIDTH), BF16),
            pltpu.VMEM((TEXTS, WIDTH), F32),
            pltpu.VMEM((SLOTS, WIDTH), F32),
            pltpu.VMEM((blocks, ROWS, WIDTH), BF16),
            pltpu.VMEM((blocks, ROWS, WIDTH), BF16),
            pltpu.VMEM((NH, 6, HALF, WIDTH), BF16),
            pltpu.VMEM((NH, 6, HALF, WIDTH), BF16),
            pltpu.VMEM((ROWS, WIDTH), BF16),
            pltpu.VMEM((ROWS, WIDTH), BF16),
            dma((2, BUCKETS)),
            dma((2, BUCKETS)),
            dma((2, BUCKETS)),
            dma((2, BUCKETS)),
            dma((2, 17)),
            dma((2, blocks)),
            dma((2, 6 * NH)),
            dma((2, 1)),
            dma((2,)),
        ],
        compiler_params=pltpu.CompilerParams(
            collective_id=0, has_side_effects=True, vmem_limit_bytes=56 << 20
        ),
    )(images, texts, owners.reshape(1, PACK), labels, counts, scale, bias)
    columns = lambda rows: pl.BlockSpec((rows, COLUMNS), lambda i: (0, i))
    grads, loss, text_grads = pl.pallas_call(
        finish,
        grid=(WIDTH // COLUMNS,),
        out_shape=(
            jax.ShapeDtypeStruct((PACK, WIDTH), BF16),
            jax.ShapeDtypeStruct((PACK,), BF16),
            jax.ShapeDtypeStruct((ROWS, WIDTH), BF16),
        ),
        in_specs=[
            columns(SLOTS),
            pl.BlockSpec((PACK, SLOTS), lambda i: (0, 0)),
            pl.BlockSpec((1, PACK), lambda i: (0, 0)),
            columns(ROWS),
        ],
        out_specs=(columns(PACK), pl.BlockSpec((PACK,), lambda i: (0,)), columns(ROWS)),
        compiler_params=pltpu.CompilerParams(vmem_limit_bytes=60 << 20),
    )(back, pick, losses, sums)
    return grads, loss, text_grads


def solution(mesh):
    rows = P(("dp", "blk"), None)
    line = P(("dp", "blk"))
    return jax.shard_map(
        body,
        mesh=mesh,
        in_specs=(rows, rows, rows, line, line, P(), P()),
        out_specs=(rows, line, rows),
        check_vma=False,
    )
```

```python
import functools

import jax
import jax.numpy as jnp
from jax import lax
from jax.experimental import pallas as pl
from jax.experimental.pallas import tpu as pltpu
from jax.sharding import PartitionSpec as P

MESH = pl.DeviceIdType.MESH
BF16 = jnp.bfloat16
F32 = jnp.float32
EPS = 1e-06

NZ, NY, NH, NX = 8, 2, 2, 4
PACK = 384
ROWS = 128
CAP = 48
BUCKETS = 16
SLOTS = CAP * BUCKETS
WIDTH = 1152
TEXTS = 2048
GROUP = 256
GROUPS = SLOTS // GROUP
HALF = ROWS // 2
COLUMNS = 1152

ORDER = (
    (0, 0), (0, 1), (1, 0), (7, 0), (1, 1), (7, 1),
    (2, 0), (6, 0), (2, 1), (6, 1), (3, 0),
    (5, 0), (3, 1), (5, 1), (4, 0), (4, 1),
)
SENT = range(1, BUCKETS)
BATCHES = (SENT[:7], SENT[7:11], SENT[11:])
LEFT = (SENT[:4], SENT[4:7], SENT[7:])


def place_of():
    p, c = lax.axis_index("dp"), lax.axis_index("blk")
    return p // NY, p % NY, c // (2 * NX), (c // 2) % NX, c % 2


def peer(dz=0, dy=0, dh=0, dx=0, dc=0):
    z, y, h, x, core = place_of()
    return (
        ((z + dz) % NZ) * NY + (y + dy) % NY,
        (((h + dh) % NH) * NX + (x + dx) % NX) * 2 + (core + dc) % 2,
    )


def block_index(dh, dx, dc):
    return (dh * 2 + dc) * NX + dx


def dot(a, b, dims):
    return lax.dot_general(a, b, ((dims[:1], dims[1:]), ((), ())), preferred_element_type=F32)


def spread():
    lane = lax.broadcasted_iota(jnp.int32, (128, SLOTS), 1)
    row = lax.broadcasted_iota(jnp.int32, (128, SLOTS), 0)
    return jnp.where(lane % CAP == row, 1.0, 0.0).astype(BF16)


def own_lanes(every):
    lane = lax.broadcasted_iota(jnp.int32, (128, SLOTS), 1)
    row = lax.broadcasted_iota(jnp.int32, (128, SLOTS), 0)
    own = lane // CAP == row // 8
    return own if every else own & (row % 8 == 0)


def pack_row(row, spreader):
    kept = jnp.where(own_lanes(True), row, 0.0).astype(BF16)
    return dot(kept, spreader, (1, 1)).reshape(BUCKETS, 8, 128)


def unpack_row(tiles, spreader):
    wide = dot(tiles.reshape(128, 128).astype(BF16), spreader, (1, 0))
    return jnp.sum(jnp.where(own_lanes(False), wide, 0.0), axis=0, keepdims=True)


def kernel(
    img_hbm, txt_hbm, own_ref, lab_ref, cnt_ref, scale_ref, bias_ref,
    back_ref, pick_hbm, loss_hbm, tgrad_hbm,
    img_ref, txt_ref, pick_ref, pick_t_ref, out_ref, recv_ref, unit_ref, coef_ref, gsend_ref,
    tagsend_ref, tagrecv_ref, losssend_ref, lossback_ref,
    texts_ref, tsum_ref, isum_ref, loss_ref, tgrad_ref,
    sibsend_ref, sibrecv_ref, xsend_ref, xrecv_ref, ysend_ref, yrecv_ref,
    img_sems, tag_sems, back_sems, lback_sems, txt_sems, sib_sems, x_sems, y_sems, local_sems,
):
    temper, offset, live_rows = scale_ref[0], bias_ref[0], cnt_ref[0]

    barrier = pltpu.get_barrier_semaphore()
    greeted = [peer(dz=ORDER[o][0], dy=ORDER[o][1]) for o in SENT]
    greeted += [peer(dc=1), peer(dh=1), peer(dx=1), peer(dx=3)]
    for device in greeted:
        pl.semaphore_signal(barrier, inc=1, device_id=device, device_id_type=MESH)
    img_load = pltpu.make_async_copy(img_hbm, img_ref, local_sems.at[0])
    txt_load = pltpu.make_async_copy(txt_hbm, txt_ref, local_sems.at[1])
    img_load.start()
    txt_load.start()

    def remote(src, dst, sems, index, device):
        return pltpu.make_async_remote_copy(
            src_ref=src,
            dst_ref=dst,
            send_sem=sems.at[0, index],
            recv_sem=sems.at[1, index],
            device_id=device,
            device_id_type=MESH,
        )

    bucket = lax.broadcasted_iota(jnp.int32, (BUCKETS, PACK), 0)
    owner_of = jnp.zeros((BUCKETS, PACK), jnp.int32)
    for o, (dz, dy) in enumerate(ORDER):
        owner_of = jnp.where(bucket == o, peer(dz=dz, dy=dy)[0], owner_of)
    live = lax.broadcasted_iota(jnp.int32, (BUCKETS, PACK), 1) < live_rows
    onehot = jnp.where((own_ref[...] == owner_of) & live, 1.0, 0.0)
    earlier = jnp.where(
        lax.broadcasted_iota(jnp.int32, (PACK, PACK), 0)
        < lax.broadcasted_iota(jnp.int32, (PACK, PACK), 1),
        1.0,
        0.0,
    ).astype(BF16)
    before = dot(onehot.astype(BF16), earlier, (1, 0))
    target = jnp.sum(onehot * (before + (bucket * CAP + 1).astype(F32)), axis=0, keepdims=True)
    target = target.astype(jnp.int32) - 1
    slot = lax.broadcasted_iota(jnp.int32, (SLOTS, PACK), 0)
    pick_ref[...] = jnp.where(slot == target, 1.0, 0.0).astype(BF16)
    spreader = spread()
    tags = dot(
        jnp.broadcast_to((lab_ref[...].reshape(1, PACK) + 1).astype(F32), (8, PACK)).astype(BF16),
        pick_ref[...],
        (1, 1),
    )
    tagsend_ref[...] = pack_row(tags[0:1], spreader)
    tagrecv_ref[0] = tagsend_ref[0]

    def bucket_rows(o):
        return pl.ds(CAP * o, CAP)

    def away(o):
        return peer(dz=ORDER[o][0], dy=ORDER[o][1])

    def home(o):
        return peer(dz=-ORDER[o][0], dy=ORDER[o][1])

    img_copies, tag_copies, back_copies, lback_copies = {}, {}, {}, {}
    for o in SENT:
        rows = bucket_rows(o)
        img_copies[o] = remote(out_ref.at[rows], recv_ref.at[rows], img_sems, o, away(o))
        tag_copies[o] = remote(tagsend_ref.at[o], tagrecv_ref.at[o], tag_sems, o, away(o))
        back_copies[o] = remote(gsend_ref.at[rows], back_ref.at[rows], back_sems, o, home(o))
        lback_copies[o] = remote(losssend_ref.at[o], lossback_ref.at[o], lback_sems, o, home(o))

    img_load.wait()
    out_ref[...] = dot(pick_ref[...], img_ref[...], (1, 0)).astype(BF16)
    txt_load.wait()
    wide = txt_ref[...].astype(F32)
    texts_ref[pl.ds(0, ROWS), :] = (
        wide * lax.rsqrt(jnp.sum(wide * wide, axis=1, keepdims=True) + EPS)
    ).astype(BF16)
    pl.semaphore_wait(barrier, len(greeted))
    for o in SENT:
        tag_copies[o].start()
    for o in BATCHES[0]:
        img_copies[o].start()

    def text_rows(dh, dx, dc, first=0, count=ROWS):
        return texts_ref.at[pl.ds(ROWS * block_index(dh, dx, dc) + first, count)]

    text_copies = {}

    def text_send(key, src, dst, device):
        text_copies[key] = remote(src, dst, txt_sems, len(text_copies), device)
        text_copies[key].start()

    def to_sibling(dh, dx):
        text_send(("c", dh, dx), text_rows(dh, dx, 0), text_rows(dh, dx, 1), peer(dc=1))

    def to_neighbours(dh):
        text_send(("x", dh, 3), text_rows(dh, 0, 0), text_rows(dh, 3, 0), peer(dx=1))
        text_send(("x", dh, 1), text_rows(dh, 0, 0), text_rows(dh, 1, 0), peer(dx=3))

    def relay(dh):
        text_copies["x", dh, 3].wait_recv()
        text_send(("r", dh, 0), text_rows(dh, 3, 0, 0, HALF), text_rows(dh, 2, 0, 0, HALF), peer(dx=1))
        to_sibling(dh, 3)
        text_copies["x", dh, 1].wait_recv()
        text_send(
            ("r", dh, 1), text_rows(dh, 1, 0, HALF, HALF), text_rows(dh, 2, 0, HALF, HALF), peer(dx=3)
        )
        to_sibling(dh, 1)

    def relayed(dh):
        text_copies["r", dh, 0].wait_recv()
        text_copies["r", dh, 1].wait_recv()
        to_sibling(dh, 2)

    text_send("h", text_rows(0, 0, 0), text_rows(1, 0, 0), peer(dh=1))
    to_neighbours(0)
    to_sibling(0, 0)
    recv_ref[bucket_rows(0), :] = out_ref[bucket_rows(0), :]
    pick_t_ref[...] = pick_ref[...].T
    pick_save = pltpu.make_async_copy(pick_t_ref, pick_hbm, local_sems.at[0])
    pick_save.start()
    inv, loss_sum, hits, sib_copies = {}, {}, {}, {}
    far = (2, 1, 3, 0)

    def group_rows(g):
        return pl.ds(g * GROUP, GROUP)

    def prepare(g, first, end):
        for o in range(max(first, 1), end):
            img_copies[o].wait_recv()
        wide = recv_ref[group_rows(g), :].astype(F32)
        inv[g] = lax.rsqrt(jnp.sum(wide * wide, axis=1, keepdims=True) + EPS)
        unit_ref[group_rows(g), :] = (wide * inv[g]).astype(BF16)

    def weigh(g, dh):
        half = pl.ds(dh * TEXTS // 2, TEXTS // 2)
        logit = temper * dot(texts_ref[half, :], unit_ref[group_rows(g), :], (1, 1)) + offset
        text = lax.broadcasted_iota(jnp.int32, logit.shape, 0) + dh * TEXTS // 2
        positive = text == hits["all"][:, g * GROUP : (g + 1) * GROUP]
        m = jnp.where(positive, -logit, logit)
        e = jnp.exp(-jnp.abs(m))
        one = 1.0 + e
        series = e * (1.0 - e * (0.5 - e * (1.0 / 3.0)))
        log1p = jnp.where(e < 0.015625, series, jnp.log(one))
        part_sum = jnp.sum(jnp.maximum(m, 0.0) + log1p, axis=0, keepdims=True)
        loss_sum[g] = loss_sum[g] + part_sum if g in loss_sum else part_sum
        sigmoid = jnp.where(m >= 0.0, 1.0, e) / one
        coef_ref[...] = (jnp.where(positive, -temper, temper) * sigmoid).astype(BF16)
        for dc in (1, 0):
            own = pl.ds(dc * TEXTS // 4, TEXTS // 4)
            part = pl.ds((dh * 2 + dc) * TEXTS // 4, TEXTS // 4)
            text_part = dot(coef_ref[own, :], unit_ref[group_rows(g), :], (1, 0))
            if g == 0:
                tsum_ref[part, :] = text_part
            else:
                tsum_ref[part, :] += text_part
            if g == GROUPS - 1 and dc:
                for dx in far:
                    k = dh * NX + dx
                    sibsend_ref[k] = tsum_ref[pl.ds(ROWS * block_index(dh, dx, 1), ROWS), :].astype(BF16)
                    sib_copies[k] = remote(sibsend_ref.at[k], sibrecv_ref.at[k], sib_sems, k, peer(dc=1))
                    sib_copies[k].start()
        image_part = dot(coef_ref[...], texts_ref[half, :], (0, 0))
        if dh == (1 if g == GROUPS - 1 else 0):
            isum_ref[group_rows(g), :] = image_part
        else:
            isum_ref[group_rows(g), :] += image_part

    def project(g):
        image_sum = isum_ref[group_rows(g), :]
        unit = recv_ref[group_rows(g), :].astype(F32) * inv[g]
        along = jnp.sum(unit * image_sum, axis=1, keepdims=True)
        gsend_ref[group_rows(g), :] = (inv[g] * (image_sum - unit * along)).astype(BF16)

    def complete(dh):
        for dx in range(NX):
            text_copies["c", dh, dx].wait_recv()

    def next_batch(i):
        for o in LEFT[i]:
            img_copies[o].wait_send()
        for o in BATCHES[i + 1]:
            img_copies[o].start()

    next_batch(0)
    relay(0)
    text_copies["h"].wait_recv()
    to_neighbours(1)
    to_sibling(1, 0)
    relayed(0)
    for o in SENT:
        tag_copies[o].wait_recv()
    hits["all"] = unpack_row(tagrecv_ref[...], spreader).astype(jnp.int32) - 1
    complete(0)
    prepare(0, 0, 6)
    weigh(0, 0)
    next_batch(1)
    relay(1)
    prepare(1, 6, 11)
    weigh(1, 0)
    relayed(1)
    complete(1)
    weigh(0, 1)
    project(0)
    for o in range(1, 5):
        back_copies[o].start()
    weigh(1, 1)
    project(1)
    for o in range(5, 10):
        back_copies[o].start()
    prepare(2, 11, BUCKETS)
    weigh(2, 1)
    weigh(2, 0)
    losses = jnp.concatenate([loss_sum[g] for g in range(GROUPS)], axis=1)
    losses = (losses / TEXTS).astype(BF16).astype(F32)
    losssend_ref[...] = pack_row(losses, spreader)
    for o in SENT:
        lback_copies[o].start()
    lossback_ref[0] = losssend_ref[0]
    project(2)
    for o in range(10, BUCKETS):
        back_copies[o].start()
    keep = pltpu.make_async_copy(
        gsend_ref.at[bucket_rows(0)], back_ref.at[bucket_rows(0)], local_sems.at[1]
    )
    keep.start()

    x_copies = {}

    def x_send(dh, m, value):
        xsend_ref[dh, m] = value.astype(BF16)
        device = peer(dx=3 if m % 2 else 1)
        x_copies[dh, m] = remote(xsend_ref.at[dh, m], xrecv_ref.at[dh, m], x_sems, dh * 6 + m, device)
        x_copies[dh, m].start()

    def x_received(dh, m):
        x_copies[dh, m].wait_recv()
        return xrecv_ref[dh, m].astype(F32)

    def chip_sum(dh, dx):
        k = dh * NX + dx
        sib_copies[k].wait_recv()
        total = tsum_ref[pl.ds(ROWS * block_index(dh, dx, 0), ROWS), :] + sibrecv_ref[k].astype(F32)
        return total[:HALF], total[HALF:]

    kept = {}
    for dh in (1, 0):
        low, high = chip_sum(dh, 2)
        x_send(dh, 0, low)
        x_send(dh, 1, high)
        ahead, high = chip_sum(dh, 1)
        x_send(dh, 2, high)
        low, behind = chip_sum(dh, 3)
        x_send(dh, 3, low)
        kept[dh] = chip_sum(dh, 0)
        x_send(dh, 4, ahead + x_received(dh, 0))
        x_send(dh, 5, behind + x_received(dh, 1))

    def gathered(dh):
        low, high = kept[dh]
        return jnp.concatenate(
            [
                low + x_received(dh, 3) + x_received(dh, 4),
                high + x_received(dh, 2) + x_received(dh, 5),
            ],
            axis=0,
        )

    ysend_ref[...] = gathered(1).astype(BF16)
    y_copy = remote(ysend_ref, yrecv_ref, y_sems, 0, peer(dh=1))
    y_copy.start()
    total = gathered(0)
    y_copy.wait_recv()
    total = total + yrecv_ref[...].astype(F32)
    wide = txt_ref[...].astype(F32)
    inv = lax.rsqrt(jnp.sum(wide * wide, axis=1, keepdims=True) + EPS)
    unit = wide * inv
    along = jnp.sum(unit * total, axis=1, keepdims=True)
    tgrad_ref[...] = (inv * (total - unit * along)).astype(BF16)
    tgrad_save = pltpu.make_async_copy(tgrad_ref, tgrad_hbm, local_sems.at[2])
    tgrad_save.start()

    pick_save.wait()
    keep.wait()
    y_copy.wait_send()
    for o in LEFT[2]:
        img_copies[o].wait_send()
    for copies in (text_copies, tag_copies, sib_copies, x_copies):
        for copy in copies.values():
            copy.wait_send()
    for copy in lback_copies.values():
        copy.wait()
    row = jnp.broadcast_to(unpack_row(lossback_ref[...], spreader), (8, SLOTS)).astype(BF16)
    loss_ref[...] = dot(row, pick_ref[...], (1, 0))[0:1]
    loss_save = pltpu.make_async_copy(loss_ref, loss_hbm, local_sems.at[3])
    loss_save.start()
    tgrad_save.wait()
    loss_save.wait()
    for copy in back_copies.values():
        copy.wait()


def finish(back_ref, pick_ref, losses_ref, sums_ref, grad_ref, loss_ref, tgrad_ref):
    grad_ref[...] = dot(pick_ref[...], back_ref[...], (1, 0)).astype(BF16)
    tgrad_ref[...] = sums_ref[...]
    loss_ref[...] = losses_ref[...].astype(BF16).reshape(PACK)


def body(images, texts, owners, labels, counts, scale, bias):
    vmem = pl.BlockSpec(memory_space=pltpu.VMEM)
    smem = pl.BlockSpec(memory_space=pltpu.SMEM)
    anywhere = pl.BlockSpec(memory_space=pl.ANY)
    dma = pltpu.SemaphoreType.DMA
    blocks = NH * NX
    back, pick, losses, sums = pl.pallas_call(
        kernel,
        out_shape=(
            jax.ShapeDtypeStruct((SLOTS, WIDTH), BF16),
            jax.ShapeDtypeStruct((PACK, SLOTS), BF16),
            jax.ShapeDtypeStruct((1, PACK), F32),
            jax.ShapeDtypeStruct((ROWS, WIDTH), BF16),
        ),
        in_specs=[anywhere] * 2 + [vmem] * 2 + [smem] * 3,
        out_specs=(anywhere,) * 4,
        scratch_shapes=[
            pltpu.VMEM((PACK, WIDTH), BF16),
            pltpu.VMEM((ROWS, WIDTH), BF16),
            pltpu.VMEM((SLOTS, PACK), BF16),
            pltpu.VMEM((PACK, SLOTS), BF16),
            pltpu.VMEM((SLOTS, WIDTH), BF16),
            pltpu.VMEM((SLOTS, WIDTH), BF16),
            pltpu.VMEM((SLOTS, WIDTH), BF16),
            pltpu.VMEM((TEXTS // 2, GROUP), BF16),
            pltpu.VMEM((SLOTS, WIDTH), BF16),
            pltpu.VMEM((BUCKETS, 8, 128), F32),
            pltpu.VMEM((BUCKETS, 8, 128), F32),
            pltpu.VMEM((BUCKETS, 8, 128), F32),
            pltpu.VMEM((BUCKETS, 8, 128), F32),
            pltpu.VMEM((TEXTS, WIDTH), BF16),
            pltpu.VMEM((TEXTS, WIDTH), F32),
            pltpu.VMEM((SLOTS, WIDTH), F32),
            pltpu.VMEM((1, PACK), F32),
            pltpu.VMEM((ROWS, WIDTH), BF16),
            pltpu.VMEM((blocks, ROWS, WIDTH), BF16),
            pltpu.VMEM((blocks, ROWS, WIDTH), BF16),
            pltpu.VMEM((NH, 6, HALF, WIDTH), BF16),
            pltpu.VMEM((NH, 6, HALF, WIDTH), BF16),
            pltpu.VMEM((ROWS, WIDTH), BF16),
            pltpu.VMEM((ROWS, WIDTH), BF16),
            dma((2, BUCKETS)),
            dma((2, BUCKETS)),
            dma((2, BUCKETS)),
            dma((2, BUCKETS)),
            dma((2, 17)),
            dma((2, blocks)),
            dma((2, 6 * NH)),
            dma((2, 1)),
            dma((4,)),
        ],
        compiler_params=pltpu.CompilerParams(
            collective_id=0, has_side_effects=True, vmem_limit_bytes=56 << 20
        ),
    )(images, texts, owners.reshape(1, PACK), labels, counts, scale, bias)
    columns = lambda rows: pl.BlockSpec((rows, COLUMNS), lambda i: (0, i))
    grads, loss, text_grads = pl.pallas_call(
        finish,
        grid=(WIDTH // COLUMNS,),
        out_shape=(
            jax.ShapeDtypeStruct((PACK, WIDTH), BF16),
            jax.ShapeDtypeStruct((PACK,), BF16),
            jax.ShapeDtypeStruct((ROWS, WIDTH), BF16),
        ),
        in_specs=[
            columns(SLOTS),
            pl.BlockSpec((PACK, SLOTS), lambda i: (0, 0)),
            pl.BlockSpec((1, PACK), lambda i: (0, 0)),
            columns(ROWS),
        ],
        out_specs=(columns(PACK), pl.BlockSpec((PACK,), lambda i: (0,)), columns(ROWS)),
        compiler_params=pltpu.CompilerParams(vmem_limit_bytes=60 << 20),
    )(back, pick, losses, sums)
    return grads, loss, text_grads


def solution(mesh):
    rows = P(("dp", "blk"), None)
    line = P(("dp", "blk"))
    return jax.shard_map(
        body,
        mesh=mesh,
        in_specs=(rows, rows, rows, line, line, P(), P()),
        out_specs=(rows, line, rows),
        check_vma=False,
    )
```
